128 devices in a mesh: row: 4 (over z_hi, core), col: 16 (over y, x), layer: 2 (over z_lo).
Axes of the slice: x: 4, y: 4, z: 4 (z_hi: 2, z_lo: 2; z = z_hi * 2 + z_lo), core: 2. Of those that a mesh axis runs over, the one named last changes fastest.
Arguments:
- x_blocks: bfloat16 [6, 16, 3, 16, 128, 128], P(None, 'row', None, 'col'), may hold values from -0.375 to 0.375
- present: int32 [6, 16, 3, 16], P(None, 'row', None, 'col'), may hold values 0 or 1
Outputs:
- purified: float32 [4, 16, 3, 16, 128, 128], P('layer', 'row', None, 'col')
The draws below stay inside these ranges and needn't reach their ends.
All inputs are finite; a program needn't handle non-finite values. No bound on the sum of `present` on one device may be relied on, other than what follows from the above.
Results may differ from the reference program's by a relative error of at most 0.0026.
Values may be sent and summed in bfloat16 or wider, within the bound.
A program may use at most 64 MiB of HBM per device.

```python
import jax
import jax.numpy as jnp

BLOCK = 128
CLASSES = 16
REGIONS = 4


def set_ends(values, stream_key, smallest, largest):
    place = [jax.random.randint(jax.random.fold_in(stream_key, axis), (), 0, length) for axis, length in enumerate(values.shape)]
    widest = values.shape.index(max(values.shape))
    next_to = place[:widest] + [(place[widest] + 1) % values.shape[widest]] + place[widest + 1:]
    return values.at[tuple(place)].set(smallest).at[tuple(next_to)].set(largest)


def steps_of(stream_key, dims, pieces, least, largest):
    def one(position, blocks):
        heights = jax.random.uniform(jax.random.fold_in(jax.random.fold_in(stream_key, 6), position), (blocks,), jnp.float32, least / len(pieces), largest / len(pieces))
        return jnp.repeat(jnp.exp(heights), dims[position] // blocks).reshape((-1,) + (1,) * (len(dims) - position - 1))

    level = one(*pieces[0])
    for cut in pieces[1:]:
        level = level * one(*cut)
    return level


def scatter_about(rng, shape, scale, reach, cuts=(), dtype=jnp.bfloat16):
    array = scale * jax.random.normal(rng, shape, jnp.float32)
    if cuts:
        array = array * steps_of(rng, shape, cuts, -0.22, 0.18)
    return jnp.clip(array, -reach, reach).astype(dtype)


def setup_inputs(seed: int = 0) -> dict:
    splits = jax.random.split(jax.random.key(seed), 3)
    x_blocks = scatter_about(splits[0], (REGIONS + 2, CLASSES, 3, CLASSES, BLOCK, BLOCK), 280 ** -0.5, 0.375, ((1, 4), (3, 16)))
    present = set_ends((jax.random.randint(splits[1], (REGIONS + 2, CLASSES, 3, CLASSES), 0, 4) < 3).astype(jnp.int32), jax.random.fold_in(splits[1], 1), 0, 1)
    return {"x_blocks": x_blocks, "present": present}


def multiply(left_blocks, right_blocks):
    columns_out = []
    for e_index in range(3):
        parts = []
        for d_index in range(3):
            other = e_index - d_index + 1
            if 0 <= other <= 2:
                left_part = left_blocks[:, :, d_index].astype(jnp.float32)
                right_part = right_blocks[d_index:d_index + REGIONS, :, other].astype(jnp.float32)
                parts.append(jnp.einsum("bacxy,bcwyz->bawxz", left_part, right_part))
        columns_out.append(jnp.sum(jnp.stack(parts), axis=0))
    return jnp.stack(columns_out, axis=2)


def reference(x_blocks, present):
    masked = x_blocks * present.astype(jnp.bfloat16)[..., None, None]
    kept_rows = present[1:REGIONS + 1].astype(jnp.float32)[..., None, None]
    square = multiply(masked[1:REGIONS + 1], masked) * kept_rows
    cubed = multiply(square.astype(jnp.bfloat16), masked) * kept_rows
    return 3.0 * square - 2.0 * cubed
```

```python
import functools

import jax
import jax.numpy as jnp
from jax import lax
from jax.experimental import pallas as pl
from jax.experimental.pallas import tpu as pltpu
from jax.sharding import PartitionSpec as P

MESH = pl.DeviceIdType.MESH
BF, F32 = jnp.bfloat16, jnp.float32
N_SEMS = 96


def kernel(
    x_ref, pres_ref, out_ref,
    xm, pmask, pmask_in, left, sq, right, sq32, acc, osend, orecv,
    send_sems, recv_sems, local_sems,
):
    row, col, zl = lax.axis_index("row"), lax.axis_index("col"), lax.axis_index("layer")
    zh, co = row // 2, row % 2
    y, x = col // 4, col % 4
    z = 2 * zh + zl

    def flip1(v):
        return v + 1 - 2 * (v % 2)

    def flip2(v):
        return (v + 2) % 4

    def flip3(v):
        return 3 - v

    def device(z_, y_, x_, co_):
        return (2 * (z_ // 2) + co_, 4 * y_ + x_, z_ % 2)

    xi = device(z, y, flip1(x), co)
    xo = device(z, y, flip3(x), co)
    y1 = device(z, flip1(y), x, co)
    y3 = device(z, flip3(y), x, co)
    zo = device(flip3(z), y, x, co)
    z2 = device(flip2(z), y, x, co)
    sib = device(z, y, x, 1 - co)
    partners = (xi, xo, y1, y3, zo, z2, sib)

    barrier = pltpu.get_barrier_semaphore()
    for partner in partners:
        pl.semaphore_signal(barrier, inc=1, device_id=partner, device_id_type=MESH)

    beta = ((x + 1) // 2) % 2
    b = 2 * zl + beta
    b_xi = 2 * zl + 1 - beta
    b_zo = 2 * (1 - zl) + beta
    my_col = 4 * y + x
    pair_col = 4 * y + flip1(x)
    my_kg = row
    zo_kg = 2 * (1 - zh) + co

    def mask_region(q, carry):
        for a in range(4):
            for o in range(3):
                kept = pres_ref[q * 12 + a * 3 + o].astype(F32)
                xm[q, a, o] = (x_ref[q, a, o].astype(F32) * kept).astype(BF)
                pmask[q, a * 3 + o] = jnp.full((128,), 1.0, F32) * kept
        for i in range(12, 16):
            pmask[q, i] = jnp.zeros((128,), F32)
        return carry

    lax.fori_loop(0, 6, mask_region, 0)
    pl.semaphore_wait(barrier, len(partners))

    started = []

    def send(src, dst, to):
        i = len(started)
        copy = pltpu.make_async_remote_copy(
            src_ref=src, dst_ref=dst, send_sem=send_sems.at[i], recv_sem=recv_sems.at[i],
            device_id=to, device_id_type=MESH,
        )
        copy.start()
        started.append(copy)
        return copy

    def gather(buf, r0, nr, p_src, q_ready):
        half = nr // 2
        full = pl.ds(r0, nr)
        part_a, part_b = pl.ds(r0, half), pl.ds(r0 + half, half)
        y1c, y2c, y3c = 4 * flip1(y), 4 * flip2(y), 4 * flip3(y)
        yc = 4 * y
        d0, d1, d2, d3 = x, flip1(x), flip2(x), flip3(x)

        def piece(c, rows, to):
            ref = buf.at[c, rows]
            return send(ref, ref, to)

        def own(to):
            return send(p_src, buf.at[my_col, full], to)

        p_xo, p_y1, p_y3 = own(xo), own(y1), own(y3)
        yield
        q_ready()
        q_y1, q_y3, q_xo = (piece(pair_col, full, t) for t in (y1, y3, xo))
        yield
        p_xo.wait_recv()
        r_y1, r_y3 = piece(yc + d3, full, y1), piece(yc + d3, full, y3)
        p_y1.wait_recv()
        p_a = piece(y1c + d0, part_a, y3)
        p_y3.wait_recv()
        p_b = piece(y3c + d0, part_b, y1)
        yield
        q_y1.wait_recv()
        q_a, s_1 = piece(y1c + d1, part_a, y3), piece(y1c + d1, full, xo)
        q_y3.wait_recv()
        q_b, s_3 = piece(y3c + d1, part_b, y1), piece(y3c + d1, full, xo)
        yield
        r_y1.wait_recv()
        r_a = piece(y1c + d3, part_a, y3)
        r_y3.wait_recv()
        r_b = piece(y3c + d3, part_b, y1)
        yield
        q_a.wait_recv()
        s_a = piece(y2c + d1, part_a, xo)
        q_b.wait_recv()
        s_b = piece(y2c + d1, part_b, xo)
        yield
        for copy in (p_a, p_b, q_xo, r_a, r_b, s_1, s_3, s_a, s_b):
            copy.wait_recv()

    def finish(stages):
        for _ in stages:
            pass

    l_xi = send(xm.at[b_xi + 1], left.at[my_col], xi)
    mask_xi = send(pmask.at[b_xi + 1], pmask_in, xi)
    z_mid = send(xm.at[b_zo + 1], right.at[0, my_kg, 1], zo)
    panel = gather(left, 0, 4, xm.at[b + 1], l_xi.wait_recv)
    next(panel)
    z_low = send(xm.at[b_zo], right.at[0, my_kg, 0], zo)
    z_high = send(xm.at[b_zo + 2], right.at[0, my_kg, 2], zo)
    c_own = send(xm.at[pl.ds(b, 3)], right.at[0, my_kg], sib)
    own_left = pltpu.make_async_copy(xm.at[b + 1], left.at[my_col], local_sems.at[0])
    own_left.start()
    own_right = pltpu.make_async_copy(xm.at[pl.ds(b, 3)], right.at[0, my_kg], local_sems.at[1])
    own_right.start()
    next(panel)
    two_xi = send(xm.at[pl.ds(b_xi + 1 - beta, 2)], right.at[1, my_kg, pl.ds(1 - beta, 2)], xi)
    one_xi = send(xm.at[b_xi + 2 * beta], right.at[1, my_kg, 2 * beta], xi)
    next(panel)
    z_mid.wait_recv()
    c_mid = send(right.at[0, zo_kg, 1], right.at[0, zo_kg, 1], sib)
    diag_xi = send(right.at[0, zo_kg, 1], right.at[1, zo_kg, 2 * beta], xi)
    next(panel)
    next(panel)
    two = right.at[1, my_kg, pl.ds(beta, 2)]
    two_xi.wait_recv()
    diag_z = send(two, two, z2)
    c_two = send(two, two, sib)
    next(panel)
    z_low.wait_recv()
    c_low = send(right.at[0, zo_kg, 0], right.at[0, zo_kg, 0], sib)
    z_high.wait_recv()
    c_high = send(right.at[0, zo_kg, 2], right.at[0, zo_kg, 2], sib)
    one_at = right.at[1, my_kg, 2 - 2 * beta]
    one_xi.wait_recv()
    c_one = send(one_at, one_at, sib)
    diag_at = right.at[1, zo_kg, 2 - 2 * beta]
    diag_xi.wait_recv()
    c_diag_xi = send(diag_at, diag_at, sib)
    zdiag_at = right.at[1, zo_kg, pl.ds(beta, 2)]
    diag_z.wait_recv()
    c_diag_z = send(zdiag_at, zdiag_at, sib)
    finish(panel)
    own_left.wait()
    own_right.wait()
    mask_xi.wait_recv()
    for copy in (c_own, c_mid, c_two, c_low, c_high, c_one, c_diag_xi, c_diag_z):
        copy.wait_recv()

    def product(buf, r0):
        for e in range(3):
            offsets = [d for d in range(3) if 0 <= e - d + 1 <= 2]

            def group(kg, carry):
                lhs = jnp.concatenate(
                    [
                        buf[4 * kg + k, r0 : r0 + 2, d].reshape(256, 128)
                        for d in offsets for k in range(4)
                    ],
                    axis=1,
                )
                rhs = jnp.concatenate(
                    [
                        jnp.concatenate([right[j, kg, d, k, e - d + 1] for j in range(2)], axis=1)
                        for d in offsets for k in range(4)
                    ],
                    axis=0,
                )
                acc[e] += jnp.dot(lhs, rhs, preferred_element_type=F32)
                return carry

            acc[e] = jnp.zeros((256, 256), F32)
            lax.fori_loop(0, 4, group, 0)

    def kept(j, a, e):
        i = a * 3 + e
        return (pmask[b + 1, i : i + 1] if j == 0 else pmask_in[i : i + 1])

    def square_rows(r0):
        product(left, r0)
        for a in range(2):
            for e in range(3):
                for j, c in ((0, my_col), (1, pair_col)):
                    block = acc[e, a * 128 : a * 128 + 128, j * 128 : j * 128 + 128]
                    block = block * kept(j, r0 + a, e)
                    sq32[j, r0 + a, e] = block
                    sq[c, r0 + a, e] = block.astype(BF)

    def result_rows(r0):
        product(sq, r0)
        for a in range(2):
            for e in range(3):
                for j in range(2):
                    block = acc[e, a * 128 : a * 128 + 128, j * 128 : j * 128 + 128]
                    block = 3.0 * sq32[j, r0 + a, e] - 2.0 * (block * kept(j, r0 + a, e))
                    if j == 0:
                        out_ref[beta, r0 + a, e] = block.astype(BF)
                    else:
                        osend[r0 + a, e] = block.astype(BF)
        return send(osend.at[pl.ds(r0, 2)], orecv.at[pl.ds(r0, 2)], xi)

    gathers = []
    for r0 in (0, 2):
        square_rows(r0)
        stages = gather(sq, r0, 2, sq.at[my_col, pl.ds(r0, 2)], lambda: None)
        next(stages)
        next(stages)
        gathers.append(stages)
    first, second = gathers
    next(first)
    next(first)
    next(second)
    next(first)
    next(first)
    next(second)
    finish(first)
    next(second)
    out_first = result_rows(0)
    finish(second)
    out_second = result_rows(2)
    for r0, copy in ((0, out_first), (2, out_second)):
        copy.wait_recv()
        out_ref[1 - beta, r0 : r0 + 2] = orecv[r0 : r0 + 2]
    for copy in started:
        copy.wait_send()


def local(x_blocks, present):
    block = jax.ShapeDtypeStruct
    x = x_blocks.reshape(6, 4, 3, 128, 128)
    purified = pl.pallas_call(
        kernel,
        out_shape=block((2, 4, 3, 128, 128), BF),
        in_specs=[pl.BlockSpec(memory_space=pltpu.VMEM), pl.BlockSpec(memory_space=pltpu.SMEM)],
        out_specs=pl.BlockSpec(memory_space=pltpu.VMEM),
        scratch_shapes=[
            pltpu.VMEM((6, 4, 3, 128, 128), BF),
            pltpu.VMEM((6, 16, 128), F32),
            pltpu.VMEM((16, 128), F32),
            pltpu.VMEM((16, 4, 3, 128, 128), BF),
            pltpu.VMEM((16, 4, 3, 128, 128), BF),
            pltpu.VMEM((2, 4, 3, 4, 3, 128, 128), BF),
            pltpu.VMEM((2, 4, 3, 128, 128), F32),
            pltpu.VMEM((3, 256, 256), F32),
            pltpu.VMEM((4, 3, 128, 128), BF),
            pltpu.VMEM((4, 3, 128, 128), BF),
            pltpu.SemaphoreType.DMA((N_SEMS,)),
            pltpu.SemaphoreType.DMA((N_SEMS,)),
            pltpu.SemaphoreType.DMA((2,)),
        ],
        compiler_params=pltpu.CompilerParams(
            collective_id=0, has_side_effects=True, vmem_limit_bytes=56 * 2**20
        ),
        cost_estimate=pl.CostEstimate(flops=7_500_000_000, bytes_accessed=4_000_000, transcendentals=0),
    )(x, present.reshape(72))
    return purified.astype(F32).reshape(2, 4, 3, 1, 128, 128)


def solution(mesh):
    return jax.shard_map(
        local,
        mesh=mesh,
        in_specs=(P(None, "row", None, "col", None, None), P(None, "row", None, "col")),
        out_specs=P("layer", "row", None, "col", None, None),
        check_vma=False,
    )
```

```python
import jax
import jax.numpy as jnp
from jax import lax
from jax.experimental import pallas as pl
from jax.experimental.pallas import tpu as pltpu
from jax.sharding import PartitionSpec as P

MESH = pl.DeviceIdType.MESH
BF, F32 = jnp.bfloat16, jnp.float32
N_SEMS = 96
C0, C1, C2, C3 = 0, 1, 2, 3


def kernel(
    x_ref, pres_ref, out_ref,
    xr, pmask, pmask_in, left, sq, right, sq32, acc_a, acc_b, acc_c, cube, osend, orecv,
    send_sems, recv_sems, local_sems,
):
    row, col, zl = lax.axis_index("row"), lax.axis_index("col"), lax.axis_index("layer")
    zh, co = row // 2, row % 2
    y, x = col // 4, col % 4
    z = 2 * zh + zl

    def flip1(v):
        return v + 1 - 2 * (v % 2)

    def flip2(v):
        return (v + 2) % 4

    def flip3(v):
        return 3 - v

    def device(z_, y_, x_, co_):
        return (2 * (z_ // 2) + co_, 4 * y_ + x_, z_ % 2)

    columns = (x, flip1(x), flip2(x), flip3(x))
    y1c, y2c, y3c = flip1(y), flip2(y), flip3(y)
    xi, x2, xo = (device(z, y, c, co) for c in columns[1:])
    y1 = device(z, y1c, x, co)
    y3 = device(z, y3c, x, co)
    zo = device(flip3(z), y, x, co)
    z2 = device(flip2(z), y, x, co)
    sib = device(z, y, x, 1 - co)
    partners = (xi, x2, xo, y1, y3, zo, z2, sib)

    barrier = pltpu.get_barrier_semaphore()
    for partner in partners:
        pl.semaphore_signal(barrier, inc=1, device_id=partner, device_id_type=MESH)

    beta, rho = x // 2, x % 2
    b = 2 * zl + beta
    b_xo = 2 * zl + 1 - beta
    b_zo = 2 * (1 - zl) + beta
    rows = 2 * rho
    rows_flip = 2 - rows
    kg0 = row
    kg1 = 2 * (1 - zh) + co
    m_at, e_at = 3 * (1 - beta), 4 * beta
    m_xo, e_xo = 3 * beta, 4 * (1 - beta)

    def mask_region(q, carry):
        for a in range(4):
            for o in range(3):
                keep = pres_ref[q * 12 + a * 3 + o].astype(F32)
                xr[3 * q + o, a] = (x_ref[q, a, o].astype(F32) * keep).astype(BF)
                pmask[q, a * 3 + o] = jnp.full((128,), 1.0, F32) * keep
        for i in range(12, 16):
            pmask[q, i] = jnp.zeros((128,), F32)
        return carry

    lax.fori_loop(0, 6, mask_region, 0)
    pl.semaphore_wait(barrier, len(partners))

    started = []

    def send(src, dst, to):
        i = len(started)
        copy = pltpu.make_async_remote_copy(
            src_ref=src, dst_ref=dst, send_sem=send_sems.at[i], recv_sem=recv_sems.at[i],
            device_id=to, device_id_type=MESH,
        )
        copy.start()
        started.append(copy)
        return copy

    def same(ref, to):
        return send(ref, ref, to)

    class Ring:
        def __init__(self, buf, j, src=None):
            self.buf, self.c = buf, columns[j]
            at = buf.at[4 * y + self.c]
            src = at if src is None else src
            self.y1, self.y3 = send(src, at, y1), send(src, at, y3)

        def relay(self):
            self.y1.wait_recv()
            self.a = same(self.buf.at[4 * y1c + self.c, :, pl.ds(0, 1)], y3)
            self.y3.wait_recv()
            self.b = same(self.buf.at[4 * y3c + self.c, :, pl.ds(1, 1)], y1)

        def wait(self):
            self.a.wait_recv()
            self.b.wait_recv()

    def left_of(region, first_row):
        return xr.at[pl.ds(3 * region + 3, 3), pl.ds(first_row, 2)]

    my_left = left.at[4 * y + x]
    own_left_src = left_of(b, rows)
    lp1 = send(left_of(b, rows_flip), my_left, xi)
    lp3 = send(left_of(b_xo, rows_flip), my_left, xo)
    lp2 = send(left_of(b_xo, rows), my_left, x2)
    l0 = Ring(left, C0, own_left_src)
    own_left = pltpu.make_async_copy(own_left_src, my_left, local_sems.at[0])
    own_left.start()

    def native(region, at, size):
        return xr.at[pl.ds(3 * region + 1 + at, size)]

    def panel(j, kg, at=None, size=7):
        return right.at[j, kg] if at is None else right.at[j, kg, pl.ds(at, size)]

    b_m = send(native(b_zo, m_at, 4), panel(C0, kg0, m_at, 4), zo)
    b_e = send(native(b_zo, e_at, 3), panel(C0, kg0, e_at, 3), zo)
    c_e = send(native(b_xo, e_xo, 3), panel(C3, kg0, e_xo, 3), xo)
    a_7 = send(native(b, 0, 7), panel(C1, kg0), xi)
    sib_0 = send(native(b, 0, 7), panel(C0, kg0), sib)
    own_right = pltpu.make_async_copy(native(b, 0, 7), panel(C0, kg0), local_sems.at[1])
    own_right.start()
    masks = [send(pmask.at[bb + 1], pmask_in.at[i], to) for i, (bb, to) in enumerate(((b, xi), (b_xo, x2), (b_xo, xo)))]

    lp1.wait_recv()
    l1 = Ring(left, C1)
    lp3.wait_recv()
    l3 = Ring(left, C3)
    l0.relay()
    lp2.wait_recv()
    l2 = Ring(left, C2)

    b_m.wait_recv()
    g_m = send(panel(C0, kg1, m_at, 4), panel(C3, kg1, m_xo, 4), xo)
    sib_b_m = same(panel(C0, kg1, m_at, 4), sib)
    c_e.wait_recv()
    c_m = send(native(b_xo, m_xo, 4), panel(C3, kg0, m_xo, 4), xo)
    h_e = same(panel(C3, kg0, e_at, 3), z2)
    sib_c_e = same(panel(C3, kg0, e_at, 3), sib)
    l1.relay()
    l3.relay()
    b_e.wait_recv()
    sib_b_e = same(panel(C0, kg1, e_at, 3), sib)
    l2.relay()
    a_7.wait_recv()
    d_7 = same(panel(C1, kg0), z2)
    f_m = send(panel(C1, kg0, m_at, 4), panel(C2, kg0, m_xo, 4), xo)
    sib_a = same(panel(C1, kg0), sib)
    g_m.wait_recv()
    i_m = send(panel(C3, kg1, m_at, 4), panel(C2, kg1, m_at, 4), xi)
    sib_g = same(panel(C3, kg1, m_at, 4), sib)
    e_e = send(panel(C3, kg0, e_at, 3), panel(C2, kg0, e_at, 3), xi)
    h_e.wait_recv()
    i_e = send(panel(C3, kg1, e_at, 3), panel(C2, kg1, e_at, 3), xi)
    sib_h = same(panel(C3, kg1, e_at, 3), sib)

    def square_column(j):
        def lhs(kg, d):
            return jnp.concatenate([left[4 * kg + k, d].reshape(256, 128) for k in range(4)], axis=1)

        def block(kg, g):
            return right[j, kg, g].reshape(512, 128)

        acc_a[...] = jnp.zeros_like(acc_a)
        acc_b[...] = jnp.zeros_like(acc_b)
        acc_c[...] = jnp.zeros_like(acc_c)

        def group(kg, carry):
            l_0, l_1, l_2 = lhs(kg, 0), lhs(kg, 1), lhs(kg, 2)
            r = [block(kg, g) for g in range(7)]
            acc_a[...] += jnp.dot(
                jnp.concatenate([l_0, l_1], axis=1),
                jnp.concatenate(
                    [jnp.concatenate([r[0], r[1]], axis=1), jnp.concatenate([r[2], r[3]], axis=1)], axis=0
                ),
                preferred_element_type=F32,
            )
            acc_b[...] += jnp.dot(l_2, jnp.concatenate([r[5], r[6]], axis=1), preferred_element_type=F32)
            acc_c[...] += jnp.dot(l_1, r[4], preferred_element_type=F32)
            return carry

        lax.fori_loop(0, 4, group, 0)
        out = (
            acc_a[:, :128],
            acc_a[:, 128:] + acc_b[:, :128],
            acc_b[:, 128:] + acc_c[...],
        )
        for e in range(3):
            for a in range(2):
                block = out[e][a * 128 : a * 128 + 128] * kept(j, a, e)
                sq32[j, e, a] = block
                sq[4 * y + columns[j], e, a] = block.astype(BF)
        return Ring(sq, j)

    def kept(j, a, e):
        i = (rows + a) * 3 + e
        return pmask[b + 1, pl.ds(i, 1)] if j == 0 else pmask_in[j - 1, pl.ds(i, 1)]

    def cube_part(j, first):
        c = columns[j]
        for e in range(3):
            offsets = [d for d in range(3) if 0 <= e - d + 1 <= 2]
            lhs = jnp.concatenate(
                [sq[4 * yy + c, d].reshape(256, 128) for d in offsets for yy in range(4)], axis=1
            )
            for half in range(2):
                rhs = jnp.concatenate(
                    [
                        jnp.concatenate([right[2 * half + i, yy, 2 * d + e, c] for i in range(2)], axis=1)
                        for d in offsets for yy in range(4)
                    ],
                    axis=0,
                )
                part = jnp.dot(lhs, rhs, preferred_element_type=F32)
                if first:
                    cube[e, half] = part
                else:
                    cube[e, half] += part

    for copy in masks:
        copy.wait_recv()
    l0.wait()
    l1.wait()
    l3.wait()
    l2.wait()
    own_left.wait()
    own_right.wait()
    for copy in (sib_0, sib_b_m, sib_b_e):
        copy.wait_recv()
    s0 = square_column(C0)
    c_m.wait_recv()
    sib_c_m = same(panel(C3, kg0, m_at, 4), sib)
    for copy in (sib_g, sib_h, sib_c_e, sib_c_m):
        copy.wait_recv()
    s3 = square_column(C3)
    s0.relay()
    d_7.wait_recv()
    sib_d = same(panel(C1, kg1), sib)
    f_m.wait_recv()
    sib_f = same(panel(C2, kg0, m_at, 4), sib)
    sib_a.wait_recv()
    sib_d.wait_recv()
    s1 = square_column(C1)
    s3.relay()
    i_m.wait_recv()
    sib_i_m = same(panel(C2, kg1, m_at, 4), sib)
    e_e.wait_recv()
    sib_e = same(panel(C2, kg0, e_at, 3), sib)
    i_e.wait_recv()
    sib_i_e = same(panel(C2, kg1, e_at, 3), sib)
    for copy in (sib_f, sib_e, sib_i_m, sib_i_e):
        copy.wait_recv()
    s2 = square_column(C2)
    s1.relay()
    s0.wait()
    cube_part(C0, True)
    s2.relay()
    s3.wait()
    cube_part(C3, False)
    s1.wait()
    cube_part(C1, False)
    s2.wait()
    cube_part(C2, False)

    outs = []
    for j in (2, 1, 3, 0):
        for e in range(3):
            for a in range(2):
                block = cube[e, j // 2, a * 128 : a * 128 + 128, (j % 2) * 128 : (j % 2) * 128 + 128]
                block = 3.0 * sq32[j, e, a] - 2.0 * (block * kept(j, a, e))
                osend[j, a, e] = block.astype(BF)
        if j:
            to = (None, xi, x2, xo)[j]
            outs.append(send(osend.at[j], orecv.at[beta, pl.ds(rows, 2)], to))
    out_ref[beta, pl.ds(rows, 2)] = osend[0]
    for copy, bb, rr in zip(outs, (1 - beta, beta, 1 - beta), (rows, rows_flip, rows_flip)):
        copy.wait_recv()
        out_ref[bb, pl.ds(rr, 2)] = orecv[bb, pl.ds(rr, 2)]
    for copy in started:
        copy.wait_send()


def local(x_blocks, present):
    block = jax.ShapeDtypeStruct
    x = x_blocks.reshape(6, 4, 3, 128, 128)
    purified = pl.pallas_call(
        kernel,
        out_shape=block((2, 4, 3, 128, 128), BF),
        in_specs=[pl.BlockSpec(memory_space=pltpu.VMEM), pl.BlockSpec(memory_space=pltpu.SMEM)],
        out_specs=pl.BlockSpec(memory_space=pltpu.VMEM),
        scratch_shapes=[
            pltpu.VMEM((18, 4, 128, 128), BF),
            pltpu.VMEM((6, 16, 128), F32),
            pltpu.VMEM((3, 16, 128), F32),
            pltpu.VMEM((16, 3, 2, 128, 128), BF),
            pltpu.VMEM((16, 3, 2, 128, 128), BF),
            pltpu.VMEM((4, 4, 7, 4, 128, 128), BF),
            pltpu.VMEM((4, 3, 2, 128, 128), F32),
            pltpu.VMEM((256, 256), F32),
            pltpu.VMEM((256, 256), F32),
            pltpu.VMEM((256, 128), F32),
            pltpu.VMEM((3, 2, 256, 256), F32),
            pltpu.VMEM((4, 2, 3, 128, 128), BF),
            pltpu.VMEM((2, 4, 3, 128, 128), BF),
            pltpu.SemaphoreType.DMA((N_SEMS,)),
            pltpu.SemaphoreType.DMA((N_SEMS,)),
            pltpu.SemaphoreType.DMA((2,)),
        ],
        compiler_params=pltpu.CompilerParams(
            collective_id=0, has_side_effects=True, vmem_limit_bytes=56 * 2**20
        ),
        cost_estimate=pl.CostEstimate(flops=7_500_000_000, bytes_accessed=4_000_000, transcendentals=0),
    )(x, present.reshape(72))
    return purified.astype(F32).reshape(2, 4, 3, 1, 128, 128)


def solution(mesh):
    return jax.shard_map(
        local,
        mesh=mesh,
        in_specs=(P(None, "row", None, "col", None, None), P(None, "row", None, "col")),
        out_specs=P("layer", "row", None, "col", None, None),
        check_vma=False,
    )
```

```python
import jax
import jax.numpy as jnp
from jax import lax
from jax.experimental import pallas as pl
from jax.experimental.pallas import tpu as pltpu
from jax.sharding import PartitionSpec as P

MESH = pl.DeviceIdType.MESH
BF, F32 = jnp.bfloat16, jnp.float32
N_SEMS = 112
C0, C1, C2, C3 = 0, 1, 2, 3


def kernel(
    x_hbm, pres_ref, out_ref,
    x_ref, xr, pmask, pmask_in, left, sq, right, sq32, acc_a, acc_b, acc_c, cube, osend,
    send_sems, recv_sems, local_sems,
):
    row, col, zl = lax.axis_index("row"), lax.axis_index("col"), lax.axis_index("layer")
    zh, co = row // 2, row % 2
    y, x = col // 4, col % 4
    z = 2 * zh + zl

    def flip1(v):
        return v + 1 - 2 * (v % 2)

    def flip2(v):
        return (v + 2) % 4

    def flip3(v):
        return 3 - v

    def device(z_, y_, x_, co_):
        return (2 * (z_ // 2) + co_, 4 * y_ + x_, z_ % 2)

    columns = (x, flip1(x), flip2(x), flip3(x))
    y1c, y2c, y3c = flip1(y), flip2(y), flip3(y)
    xi, x2, xo = (device(z, y, c, co) for c in columns[1:])
    y1 = device(z, y1c, x, co)
    y3 = device(z, y3c, x, co)
    zo = device(flip3(z), y, x, co)
    z2 = device(flip2(z), y, x, co)
    sib = device(z, y, x, 1 - co)
    partners = (xi, x2, xo, y1, y3, zo, z2, sib)

    x_in = pltpu.make_async_copy(x_hbm, x_ref, local_sems.at[2])
    x_in.start()
    barrier = pltpu.get_barrier_semaphore()
    for partner in partners:
        pl.semaphore_signal(barrier, inc=1, device_id=partner, device_id_type=MESH)

    beta, rho = x // 2, x % 2
    b = 2 * zl + beta
    b_xo = 2 * zl + 1 - beta
    b_zo = 2 * (1 - zl) + beta
    rows = 2 * rho
    rows_flip = 2 - rows
    kg0 = row
    kg1 = 2 * (1 - zh) + co
    m_at, e_at = 3 * (1 - beta), 4 * beta
    m_xo, e_xo = 3 * beta, 4 * (1 - beta)

    def mask_region(q, carry):
        for a in range(4):
            for o in range(3):
                keep = pres_ref[a, o, 0, q].astype(F32)
                xr[3 * q + o, a] = (x_ref[q, a, o].astype(F32) * keep).astype(BF)
                pmask[q, a * 3 + o] = jnp.full((128,), 1.0, F32) * keep
        for i in range(12, 16):
            pmask[q, i] = jnp.zeros((128,), F32)
        return carry

    x_in.wait()
    lax.fori_loop(0, 6, mask_region, 0)
    pl.semaphore_wait(barrier, len(partners))

    started = []

    def send(src, dst, to):
        i = len(started)
        copy = pltpu.make_async_remote_copy(
            src_ref=src, dst_ref=dst, send_sem=send_sems.at[i], recv_sem=recv_sems.at[i],
            device_id=to, device_id_type=MESH,
        )
        copy.start()
        started.append(copy)
        return copy

    def same(ref, to):
        return send(ref, ref, to)

    class Ring:
        def __init__(self, buf, c, wide=1, rows_at=0, count=2):
            self.buf, self.c, self.wide, self.rows = buf, c, wide, pl.ds(rows_at, count)
            self.y1, self.y3 = same(self.at(y), y1), same(self.at(y), y3)

        def at(self, yy, *half):
            return self.buf.at[(pl.ds(4 * yy + self.c, self.wide), slice(None), self.rows, *half)]

        def relay(self):
            self.y1.wait_recv()
            self.a = same(self.at(y1c, pl.ds(0, 64)), y3)
            self.y3.wait_recv()
            self.b = same(self.at(y3c, pl.ds(64, 64)), y1)

        def wait(self):
            self.a.wait_recv()
            self.b.wait_recv()

    def left_of(region, first_row):
        return xr.at[pl.ds(3 * region + 3, 3), pl.ds(first_row, 2)]

    my_left = left.at[4 * y + x]
    own_left_src = left_of(b, rows)
    lp1 = send(left_of(b, rows_flip), my_left, xi)
    lp3 = send(left_of(b_xo, rows_flip), my_left, xo)
    lp2 = send(left_of(b_xo, rows), my_left, x2)
    own_left = pltpu.make_async_copy(own_left_src, my_left, local_sems.at[0])
    own_left.start()

    def native(region, at, size):
        return xr.at[pl.ds(3 * region + 1 + at, size)]

    def panel(j, kg, at=None, size=7):
        return right.at[j, kg] if at is None else right.at[j, kg, pl.ds(at, size)]

    masks = [send(pmask.at[bb + 1], pmask_in.at[i], to) for i, (bb, to) in enumerate(((b, xi), (b_xo, x2), (b_xo, xo)))]
    b_m = send(native(b_zo, m_at, 4), panel(C0, kg0, m_at, 4), zo)
    c_e = send(native(b_xo, e_xo, 3), panel(C3, kg0, e_xo, 3), xo)
    a_m = send(native(b, m_at, 4), panel(C1, kg0, m_at, 4), xi)
    b_e = send(native(b_zo, e_at, 3), panel(C0, kg0, e_at, 3), zo)
    own_right = pltpu.make_async_copy(native(b, 0, 7), panel(C0, kg0), local_sems.at[1])
    own_right.start()
    own_left.wait()
    lp1.wait_recv()
    l_near = Ring(left, 2 * (x // 2), 2)
    a_e = send(native(b, e_at, 3), panel(C1, kg0, e_at, 3), xi)
    sib_0 = send(native(b, 0, 7), panel(C0, kg0), sib)
    lp3.wait_recv()
    lp2.wait_recv()
    l_far = Ring(left, 2 * (1 - x // 2), 2)
    b_m.wait_recv()
    g_m = send(panel(C0, kg1, m_at, 4), panel(C3, kg1, m_xo, 4), xo)
    sib_b_m = same(panel(C0, kg1, m_at, 4), sib)
    c_e.wait_recv()
    h_e = same(panel(C3, kg0, e_at, 3), z2)
    e_e = send(panel(C3, kg0, e_at, 3), panel(C2, kg0, e_at, 3), xi)
    c_m = send(native(b_xo, m_xo, 4), panel(C3, kg0, m_xo, 4), xo)
    sib_c_e = same(panel(C3, kg0, e_at, 3), sib)
    l_near.relay()
    b_e.wait_recv()
    sib_b_e = same(panel(C0, kg1, e_at, 3), sib)
    a_m.wait_recv()
    f_m = send(panel(C1, kg0, m_at, 4), panel(C2, kg0, m_xo, 4), xo)
    sib_a_m = same(panel(C1, kg0, m_at, 4), sib)
    l_far.relay()
    a_e.wait_recv()
    d_m = same(panel(C1, kg0, m_at, 4), z2)
    d_e = same(panel(C1, kg0, e_at, 3), z2)
    sib_a_e = same(panel(C1, kg0, e_at, 3), sib)
    g_m.wait_recv()
    i_m = send(panel(C3, kg1, m_at, 4), panel(C2, kg1, m_at, 4), xi)
    sib_g = same(panel(C3, kg1, m_at, 4), sib)

    def part(j, kg, half):
        return right.at[j, kg, pl.ds(e_at, 3), pl.ds(2 * half, 2)]

    def square_half(j, first):
        def lhs(kg, d):
            return jnp.concatenate([left[4 * kg + k, d].reshape(256, 128) for k in range(4)], axis=1)

        def block(kg, g):
            return right[j, kg, g].reshape(512, 128)

        if first:
            acc_a[...] = jnp.zeros_like(acc_a)
            acc_b[...] = jnp.zeros_like(acc_b)
            acc_c[...] = jnp.zeros_like(acc_c)
        start = 2 * zh if first else 2 * (1 - zh)

        def group(i, carry):
            kg = start + i
            l_0, l_1, l_2 = lhs(kg, 0), lhs(kg, 1), lhs(kg, 2)
            r = [block(kg, g) for g in range(7)]
            acc_a[...] += jnp.dot(
                jnp.concatenate([l_0, l_1], axis=1),
                jnp.concatenate(
                    [jnp.concatenate([r[0], r[1]], axis=1), jnp.concatenate([r[2], r[3]], axis=1)], axis=0
                ),
                preferred_element_type=F32,
            )
            acc_b[...] += jnp.dot(l_2, jnp.concatenate([r[5], r[6]], axis=1), preferred_element_type=F32)
            acc_c[...] += jnp.dot(l_1, r[4], preferred_element_type=F32)
            return carry

        lax.fori_loop(0, 2, group, 0)

    def kept(j, a, e):
        i = (rows + a) * 3 + e
        return pmask[b + 1, pl.ds(i, 1)] if j == 0 else pmask_in[j - 1, pl.ds(i, 1)]

    def square_store(j, a):
        at = slice(a * 128, a * 128 + 128)
        out = (
            acc_a[at, :128],
            acc_a[at, 128:] + acc_b[at, :128],
            acc_b[at, 128:] + acc_c[at],
        )
        for e in range(3):
            block = out[e] * kept(j, a, e)
            sq32[j, e, a] = block
            sq[4 * y + columns[j], e, a] = block.astype(BF)

    def square_column(j):
        square_half(j, True)
        square_half(j, False)
        square_store(j, 0)
        square_store(j, 1)
        return Ring(sq, columns[j])

    def cube_part(j, first=False, row_at=0, count=2, halves=(0, 1)):
        c, m = columns[j], 128 * count
        at = slice(row_at * 128, row_at * 128 + m)
        for e in range(3):
            offsets = [d for d in range(3) if 0 <= e - d + 1 <= 2]
            lhs = jnp.concatenate(
                [
                    sq[4 * yy + c, d, row_at : row_at + count].reshape(m, 128)
                    for d in offsets for yy in range(4)
                ],
                axis=1,
            )
            for half in halves:
                rhs = jnp.concatenate(
                    [
                        jnp.concatenate([right[2 * half + i, yy, 2 * d + e, c] for i in range(2)], axis=1)
                        for d in offsets for yy in range(4)
                    ],
                    axis=0,
                )
                part = jnp.dot(lhs, rhs, preferred_element_type=F32)
                if first:
                    cube[e, half, at] = part
                else:
                    cube[e, half, at] += part

    outs = []

    def result_row(a):
        for j in (2, 1, 3, 0):
            for e in range(3):
                block = cube[e, j // 2, a * 128 : a * 128 + 128, (j % 2) * 128 : (j % 2) * 128 + 128]
                block = (3.0 * sq32[j, e, a] - 2.0 * (block * kept(j, a, e))).astype(BF)
                if j:
                    osend[j, a, e] = block
                else:
                    out_ref[beta, rows + a, e] = block
            if j:
                outs.append(send(osend.at[j, a], out_ref.at[beta, rows + a], (None, xi, x2, xo)[j]))

    def arrived(*copies):
        for copy in copies:
            copy.wait_recv()

    arrived(*masks)
    l_near.wait()
    l_far.wait()
    own_right.wait()
    arrived(sib_0, sib_b_m, sib_b_e)
    s0 = square_column(C0)
    e_e.wait_recv()
    j_e = same(part(C2, kg0, 1), z2)
    sib_e = same(panel(C2, kg0, e_at, 3), sib)
    h_e.wait_recv()
    i_e = send(part(C3, kg1, 0), part(C2, kg1, 0), xi)
    sib_h = same(panel(C3, kg1, e_at, 3), sib)
    c_m.wait_recv()
    sib_c_m = same(panel(C3, kg0, m_at, 4), sib)
    s0.relay()
    arrived(sib_g, sib_h, sib_c_e, sib_c_m)
    s3 = square_column(C3)
    arrived(sib_a_m, sib_a_e)
    square_half(C1, True)
    i_m.wait_recv()
    sib_i_m = same(panel(C2, kg1, m_at, 4), sib)
    d_m.wait_recv()
    sib_d_m = same(panel(C1, kg1, m_at, 4), sib)
    s3.relay()
    d_e.wait_recv()
    sib_d_e = same(panel(C1, kg1, e_at, 3), sib)
    f_m.wait_recv()
    sib_f = same(panel(C2, kg0, m_at, 4), sib)
    arrived(sib_d_m, sib_d_e)
    square_half(C1, False)
    square_store(C1, 0)
    s1 = [Ring(sq, columns[C1], 1, 0, 1)]
    square_store(C1, 1)
    i_e.wait_recv()
    sib_i_e = same(part(C2, kg1, 0), sib)
    j_e.wait_recv()
    sib_j_e = same(part(C2, kg1, 1), sib)
    arrived(sib_f, sib_e)
    square_half(C2, True)
    arrived(sib_i_m, sib_i_e, sib_j_e)
    square_half(C2, False)
    square_store(C2, 0)
    s2 = [Ring(sq, columns[C2], 1, 0, 1)]
    square_store(C2, 1)
    s1[0].relay()
    s0.wait()
    cube_part(C0, True, halves=(0,))
    s2[0].relay()
    s1.append(Ring(sq, columns[C1], 1, 1, 1))
    s2.append(Ring(sq, columns[C2], 1, 1, 1))
    cube_part(C0, True, halves=(1,))
    s3.wait()
    cube_part(C3)
    s1[0].wait()
    cube_part(C1, False, 0, 1)
    s2[0].wait()
    cube_part(C2, False, 0, 1)
    s1[1].relay()
    s2[1].relay()
    result_row(0)
    s1[1].wait()
    cube_part(C1, False, 1, 1)
    s2[1].wait()
    cube_part(C2, False, 1, 1)
    result_row(1)
    arrived(*outs)
    for copy in started:
        copy.wait_send()


def local(x_blocks, present):
    block = jax.ShapeDtypeStruct
    x = x_blocks.reshape(6, 4, 3, 128, 128)
    purified = pl.pallas_call(
        kernel,
        out_shape=block((2, 4, 3, 128, 128), BF),
        in_specs=[pl.BlockSpec(memory_space=pl.ANY), pl.BlockSpec(memory_space=pltpu.SMEM)],
        out_specs=pl.BlockSpec(memory_space=pltpu.VMEM),
        scratch_shapes=[
            pltpu.VMEM((6, 4, 3, 128, 128), BF),
            pltpu.VMEM((18, 4, 128, 128), BF),
            pltpu.VMEM((6, 16, 128), F32),
            pltpu.VMEM((3, 16, 128), F32),
            pltpu.VMEM((16, 3, 2, 128, 128), BF),
            pltpu.VMEM((16, 3, 2, 128, 128), BF),
            pltpu.VMEM((4, 4, 7, 4, 128, 128), BF),
            pltpu.VMEM((4, 3, 2, 128, 128), F32),
            pltpu.VMEM((256, 256), F32),
            pltpu.VMEM((256, 256), F32),
            pltpu.VMEM((256, 128), F32),
            pltpu.VMEM((3, 2, 256, 256), F32),
            pltpu.VMEM((4, 2, 3, 128, 128), BF),
            pltpu.SemaphoreType.DMA((N_SEMS,)),
            pltpu.SemaphoreType.DMA((N_SEMS,)),
            pltpu.SemaphoreType.DMA((3,)),
        ],
        compiler_params=pltpu.CompilerParams(
            collective_id=0, has_side_effects=True, vmem_limit_bytes=44 * 2**20
        ),
        cost_estimate=pl.CostEstimate(flops=7_500_000_000, bytes_accessed=4_000_000, transcendentals=0),
    )(
        pltpu.with_memory_space_constraint(x, pltpu.HBM),
        pltpu.with_memory_space_constraint(present.transpose(1, 2, 3, 0), pltpu.HBM),
    )
    return purified.astype(F32).reshape(2, 4, 3, 1, 128, 128)


def solution(mesh):
    return jax.shard_map(
        local,
        mesh=mesh,
        in_specs=(P(None, "row", None, "col", None, None), P(None, "row", None, "col")),
        out_specs=P("layer", "row", None, "col", None, None),
        check_vma=False,
    )
```

```python
import jax
import jax.numpy as jnp
from jax import lax
from jax.experimental import pallas as pl
from jax.experimental.pallas import tpu as pltpu
from jax.sharding import PartitionSpec as P

MESH = pl.DeviceIdType.MESH
BF, F32 = jnp.bfloat16, jnp.float32
N_SEMS = 112
C0, C1, C2, C3 = 0, 1, 2, 3
PAIRS = ((C0, C3), (C1, C2))


def kernel(
    x_hbm, pres_ref, out_ref,
    x_ref, xr, pmask, pmask_in, left, sq, right, sq32, acc_a, acc_b, acc_c, cube, osend,
    send_sems, recv_sems, local_sems,
):
    row, col, zl = lax.axis_index("row"), lax.axis_index("col"), lax.axis_index("layer")
    zh, co = row // 2, row % 2
    y, x = col // 4, col % 4
    z = 2 * zh + zl

    def flip1(v):
        return v + 1 - 2 * (v % 2)

    def flip2(v):
        return (v + 2) % 4

    def flip3(v):
        return 3 - v

    def device(z_, y_, x_, co_):
        return (2 * (z_ // 2) + co_, 4 * y_ + x_, z_ % 2)

    columns = (x, flip1(x), flip2(x), flip3(x))
    y1c, y2c, y3c = flip1(y), flip2(y), flip3(y)
    xi, x2, xo = (device(z, y, c, co) for c in columns[1:])
    y1 = device(z, y1c, x, co)
    y3 = device(z, y3c, x, co)
    zo = device(flip3(z), y, x, co)
    z2 = device(flip2(z), y, x, co)
    sib = device(z, y, x, 1 - co)
    partners = (xi, x2, xo, y1, y3, zo, z2, sib)

    x_in = pltpu.make_async_copy(x_hbm, x_ref, local_sems.at[2])
    x_in.start()
    barrier = pltpu.get_barrier_semaphore()
    for partner in partners:
        pl.semaphore_signal(barrier, inc=1, device_id=partner, device_id_type=MESH)

    beta, rho = x // 2, x % 2
    b = 2 * zl + beta
    b_xo = 2 * zl + 1 - beta
    b_zo = 2 * (1 - zl) + beta
    rows = 2 * rho
    rows_flip = 2 - rows
    kg0 = row
    kg1 = 2 * (1 - zh) + co
    m_at, e_at = 3 * (1 - beta), 4 * beta
    m_xo, e_xo = 3 * beta, 4 * (1 - beta)

    def mask_region(q, carry):
        for a in range(4):
            for o in range(3):
                keep = pres_ref[a, o, 0, q].astype(F32)
                xr[3 * q + o, a] = (x_ref[q, a, o].astype(F32) * keep).astype(BF)
                pmask[q, a * 3 + o] = jnp.full((128,), 1.0, F32) * keep
        for i in range(12, 16):
            pmask[q, i] = jnp.zeros((128,), F32)
        return carry

    x_in.wait()
    lax.fori_loop(0, 6, mask_region, 0)
    pl.semaphore_wait(barrier, len(partners))

    started = []

    def send(src, dst, to):
        i = len(started)
        copy = pltpu.make_async_remote_copy(
            src_ref=src, dst_ref=dst, send_sem=send_sems.at[i], recv_sem=recv_sems.at[i],
            device_id=to, device_id_type=MESH,
        )
        copy.start()
        started.append(copy)
        return copy

    def same(ref, to):
        return send(ref, ref, to)

    class Ring:
        def __init__(self, buf, c, wide=1, rows_at=0, count=2):
            self.buf, self.c, self.wide, self.rows = buf, c, wide, pl.ds(rows_at, count)
            self.y1, self.y3 = same(self.at(y), y1), same(self.at(y), y3)

        def at(self, yy, *half):
            return self.buf.at[(pl.ds(4 * yy + self.c, self.wide), slice(None), self.rows, *half)]

        def relay(self):
            self.y1.wait_recv()
            self.a = same(self.at(y1c, pl.ds(0, 64)), y3)
            self.y3.wait_recv()
            self.b = same(self.at(y3c, pl.ds(64, 64)), y1)

        def wait(self):
            self.a.wait_recv()
            self.b.wait_recv()

    def left_of(region, first_row):
        return xr.at[pl.ds(3 * region + 3, 3), pl.ds(first_row, 2)]

    my_left = left.at[4 * y + x]
    own_left_src = left_of(b, rows)
    lp1 = send(left_of(b, rows_flip), my_left, xi)
    lp3 = send(left_of(b_xo, rows_flip), my_left, xo)
    lp2 = send(left_of(b_xo, rows), my_left, x2)
    own_left = pltpu.make_async_copy(own_left_src, my_left, local_sems.at[0])
    own_left.start()

    def native(region, at, size):
        return xr.at[pl.ds(3 * region + 1 + at, size)]

    def panel(j, kg, at=None, size=7):
        return right.at[j, kg] if at is None else right.at[j, kg, pl.ds(at, size)]

    masks = [send(pmask.at[bb + 1], pmask_in.at[i], to) for i, (bb, to) in enumerate(((b, xi), (b_xo, x2), (b_xo, xo)))]
    b_m = send(native(b_zo, m_at, 4), panel(C0, kg0, m_at, 4), zo)
    c_e = send(native(b_xo, e_xo, 3), panel(C3, kg0, e_xo, 3), xo)
    a_m = send(native(b, m_at, 4), panel(C1, kg0, m_at, 4), xi)
    b_e = send(native(b_zo, e_at, 3), panel(C0, kg0, e_at, 3), zo)
    own_right = pltpu.make_async_copy(native(b, 0, 7), panel(C0, kg0), local_sems.at[1])
    own_right.start()
    own_left.wait()
    lp1.wait_recv()
    l_near = Ring(left, 2 * (x // 2), 2)
    a_e = send(native(b, e_at, 3), panel(C1, kg0, e_at, 3), xi)
    sib_0 = send(native(b, 0, 7), panel(C0, kg0), sib)
    lp3.wait_recv()
    lp2.wait_recv()
    l_far = Ring(left, 2 * (1 - x // 2), 2)
    b_m.wait_recv()
    g_m = send(panel(C0, kg1, m_at, 4), panel(C3, kg1, m_xo, 4), xo)
    sib_b_m = same(panel(C0, kg1, m_at, 4), sib)
    c_e.wait_recv()
    h_e = same(panel(C3, kg0, e_at, 3), z2)
    e_e = send(panel(C3, kg0, e_at, 3), panel(C2, kg0, e_at, 3), xi)
    c_m = send(native(b_xo, m_xo, 4), panel(C3, kg0, m_xo, 4), xo)
    sib_c_e = same(panel(C3, kg0, e_at, 3), sib)
    l_near.relay()
    b_e.wait_recv()
    sib_b_e = same(panel(C0, kg1, e_at, 3), sib)
    a_m.wait_recv()
    f_m = send(panel(C1, kg0, m_at, 4), panel(C2, kg0, m_xo, 4), xo)
    sib_a_m = same(panel(C1, kg0, m_at, 4), sib)
    l_far.relay()
    a_e.wait_recv()
    d_m = same(panel(C1, kg0, m_at, 4), z2)
    d_e = same(panel(C1, kg0, e_at, 3), z2)
    sib_a_e = same(panel(C1, kg0, e_at, 3), sib)
    g_m.wait_recv()
    i_m = send(panel(C3, kg1, m_at, 4), panel(C2, kg1, m_at, 4), xi)
    sib_g = same(panel(C3, kg1, m_at, 4), sib)

    def part(j, kg, half):
        return right.at[j, kg, pl.ds(e_at, 3), pl.ds(2 * half, 2)]

    def square_half(j, first):
        def lhs(kg, d):
            return jnp.concatenate([left[4 * kg + k, d].reshape(256, 128) for k in range(4)], axis=1)

        def block(kg, g):
            return right[j, kg, g].reshape(512, 128)

        if first:
            acc_a[...] = jnp.zeros_like(acc_a)
            acc_b[...] = jnp.zeros_like(acc_b)
            acc_c[...] = jnp.zeros_like(acc_c)
        start = 2 * zh if first else 2 * (1 - zh)

        def group(i, carry):
            kg = start + i
            l_0, l_1, l_2 = lhs(kg, 0), lhs(kg, 1), lhs(kg, 2)
            r = [block(kg, g) for g in range(7)]
            acc_a[...] += jnp.dot(
                jnp.concatenate([l_0, l_1], axis=1),
                jnp.concatenate(
                    [jnp.concatenate([r[0], r[1]], axis=1), jnp.concatenate([r[2], r[3]], axis=1)], axis=0
                ),
                preferred_element_type=F32,
            )
            acc_b[...] += jnp.dot(l_2, jnp.concatenate([r[5], r[6]], axis=1), preferred_element_type=F32)
            acc_c[...] += jnp.dot(l_1, r[4], preferred_element_type=F32)
            return carry

        lax.fori_loop(0, 2, group, 0)

    def kept(j, a, e):
        i = (rows + a) * 3 + e
        return pmask[b + 1, pl.ds(i, 1)] if j == 0 else pmask_in[j - 1, pl.ds(i, 1)]

    def square_store(j, a):
        at = slice(a * 128, a * 128 + 128)
        out = (
            acc_a[at, :128],
            acc_a[at, 128:] + acc_b[at, :128],
            acc_b[at, 128:] + acc_c[at],
        )
        for e in range(3):
            block = out[e] * kept(j, a, e)
            sq32[j, e, a] = block
            sq[4 * y + columns[j], e, a] = block.astype(BF)

    def square_column(j):
        square_half(j, True)
        square_half(j, False)
        square_store(j, 0)
        square_store(j, 1)
        return Ring(sq, columns[j])

    def cube_part(j, first=False, row_at=0, count=2, halves=(0, 1), ys=(0, 1, 2, 3)):
        c, m = columns[j], 128 * count
        at = slice(row_at * 128, row_at * 128 + m)
        for e in range(3):
            offsets = [d for d in range(3) if 0 <= e - d + 1 <= 2]
            lhs = jnp.concatenate(
                [
                    sq[4 * yy + c, d, row_at : row_at + count].reshape(m, 128)
                    for d in offsets for yy in ys
                ],
                axis=1,
            )
            for half in halves:
                rhs = jnp.concatenate(
                    [
                        jnp.concatenate([right[j, yy, 2 * d + e, c] for j in PAIRS[half]], axis=1)
                        for d in offsets for yy in ys
                    ],
                    axis=0,
                )
                part = jnp.dot(lhs, rhs, preferred_element_type=F32)
                if first:
                    cube[e, half, at] = part
                else:
                    cube[e, half, at] += part

    outs = []

    def result_row(a):
        for j in (C2, C1, C3, C0):
            half = 0 if j in PAIRS[0] else 1
            at = PAIRS[half].index(j)
            for e in range(3):
                block = cube[e, half, a * 128 : a * 128 + 128, at * 128 : at * 128 + 128]
                block = (3.0 * sq32[j, e, a] - 2.0 * (block * kept(j, a, e))).astype(BF)
                if j:
                    osend[j, a, e] = block
                else:
                    out_ref[beta, rows + a, e] = block
            if j:
                outs.append(send(osend.at[j, a], out_ref.at[beta, rows + a], (None, xi, x2, xo)[j]))

    def arrived(*copies):
        for copy in copies:
            copy.wait_recv()

    arrived(*masks)
    l_near.wait()
    l_far.wait()
    own_right.wait()
    arrived(sib_0, sib_b_m, sib_b_e)
    s0 = square_column(C0)
    e_e.wait_recv()
    j_e = same(part(C2, kg0, 1), z2)
    sib_e = same(panel(C2, kg0, e_at, 3), sib)
    h_e.wait_recv()
    i_e = send(part(C3, kg1, 0), part(C2, kg1, 0), xi)
    sib_h = same(panel(C3, kg1, e_at, 3), sib)
    c_m.wait_recv()
    sib_c_m = same(panel(C3, kg0, m_at, 4), sib)
    s0.relay()
    arrived(sib_g, sib_h, sib_c_e, sib_c_m)
    s3 = square_column(C3)
    arrived(sib_a_m, sib_a_e)
    square_half(C1, True)
    s0.wait()
    cube_part(C0, True, halves=(0,))
    i_m.wait_recv()
    sib_i_m = same(panel(C2, kg1, m_at, 4), sib)
    d_m.wait_recv()
    sib_d_m = same(panel(C1, kg1, m_at, 4), sib)
    s3.relay()
    d_e.wait_recv()
    sib_d_e = same(panel(C1, kg1, e_at, 3), sib)
    arrived(sib_d_m, sib_d_e)
    square_half(C1, False)
    square_store(C1, 0)
    s1 = [Ring(sq, columns[C1], 1, 0, 1)]
    f_m.wait_recv()
    sib_f = same(panel(C2, kg0, m_at, 4), sib)
    square_store(C1, 1)
    i_e.wait_recv()
    sib_i_e = same(part(C2, kg1, 0), sib)
    j_e.wait_recv()
    sib_j_e = same(part(C2, kg1, 1), sib)
    arrived(sib_f, sib_e)
    square_half(C2, True)
    arrived(sib_i_m, sib_i_e, sib_j_e)
    square_half(C2, False)
    square_store(C2, 0)
    s2 = [Ring(sq, columns[C2], 1, 0, 1)]
    square_store(C2, 1)
    s1[0].relay()
    cube_part(C0, True, halves=(1,))
    s3.wait()
    s2[0].relay()
    s1.append(Ring(sq, columns[C1], 1, 1, 1))
    s2.append(Ring(sq, columns[C2], 1, 1, 1))
    cube_part(C3)
    s1[0].wait()
    cube_part(C1, False, 0, 1)
    cube_part(C2, False, 0, 1, ys=(y, y1c, y3c))
    s2[0].wait()
    cube_part(C2, False, 0, 1, ys=(y2c,))
    result_row(0)
    s1[1].relay()
    s2[1].relay()
    cube_part(C2, False, 1, 1, ys=(y, y1c, y3c))
    s1[1].wait()
    cube_part(C1, False, 1, 1)
    s2[1].wait()
    cube_part(C2, False, 1, 1, ys=(y2c,))
    result_row(1)
    for copy in started:
        if all(copy is not other for other in outs):
            copy.wait_send()
    for copy in outs:
        copy.wait()


def local(x_blocks, present):
    block = jax.ShapeDtypeStruct
    x = x_blocks.reshape(6, 4, 3, 128, 128)
    purified = pl.pallas_call(
        kernel,
        out_shape=block((2, 4, 3, 128, 128), BF),
        in_specs=[pl.BlockSpec(memory_space=pl.ANY), pl.BlockSpec(memory_space=pltpu.SMEM)],
        out_specs=pl.BlockSpec(memory_space=pltpu.VMEM),
        scratch_shapes=[
            pltpu.VMEM((6, 4, 3, 128, 128), BF),
            pltpu.VMEM((18, 4, 128, 128), BF),
            pltpu.VMEM((6, 16, 128), F32),
            pltpu.VMEM((3, 16, 128), F32),
            pltpu.VMEM((16, 3, 2, 128, 128), BF),
            pltpu.VMEM((16, 3, 2, 128, 128), BF),
            pltpu.VMEM((4, 4, 7, 4, 128, 128), BF),
            pltpu.VMEM((4, 3, 2, 128, 128), F32),
            pltpu.VMEM((256, 256), F32),
            pltpu.VMEM((256, 256), F32),
            pltpu.VMEM((256, 128), F32),
            pltpu.VMEM((3, 2, 256, 256), F32),
            pltpu.VMEM((4, 2, 3, 128, 128), BF),
            pltpu.SemaphoreType.DMA((N_SEMS,)),
            pltpu.SemaphoreType.DMA((N_SEMS,)),
            pltpu.SemaphoreType.DMA((3,)),
        ],
        compiler_params=pltpu.CompilerParams(
            collective_id=0, has_side_effects=True, vmem_limit_bytes=44 * 2**20
        ),
        cost_estimate=pl.CostEstimate(flops=7_500_000_000, bytes_accessed=4_000_000, transcendentals=0),
    )(
        pltpu.with_memory_space_constraint(x, pltpu.HBM),
        pltpu.with_memory_space_constraint(present.transpose(1, 2, 3, 0), pltpu.HBM),
    )
    return purified.astype(F32).reshape(2, 4, 3, 1, 128, 128)


def solution(mesh):
    return jax.shard_map(
        local,
        mesh=mesh,
        in_specs=(P(None, "row", None, "col", None, None), P(None, "row", None, "col")),
        out_specs=P("layer", "row", None, "col", None, None),
        check_vma=False,
    )
```

```python
import jax
import jax.numpy as jnp
from jax import lax
from jax.experimental import pallas as pl
from jax.experimental.pallas import tpu as pltpu
from jax.sharding import PartitionSpec as P

MESH = pl.DeviceIdType.MESH
BF, F32 = jnp.bfloat16, jnp.float32
N_SEMS = 112
C0, C1, C2, C3 = 0, 1, 2, 3
PAIRS = ((C0, C3), (C1, C2))


def kernel(
    x_hbm, pres_ref, out_ref,
    x_ref, xr, pmask, pmask_in, left, sq, right, sq32, acc_a, acc_b, acc_c, cube, osend,
    send_sems, recv_sems, local_sems,
):
    row, col, zl = lax.axis_index("row"), lax.axis_index("col"), lax.axis_index("layer")
    zh, co = row // 2, row % 2
    y, x = col // 4, col % 4
    z = 2 * zh + zl

    def flip1(v):
        return v + 1 - 2 * (v % 2)

    def flip2(v):
        return (v + 2) % 4

    def flip3(v):
        return 3 - v

    def device(z_, y_, x_, co_):
        return (2 * (z_ // 2) + co_, 4 * y_ + x_, z_ % 2)

    columns = (x, flip1(x), flip2(x), flip3(x))
    y1c, y2c, y3c = flip1(y), flip2(y), flip3(y)
    xi, x2, xo = (device(z, y, c, co) for c in columns[1:])
    y1 = device(z, y1c, x, co)
    y3 = device(z, y3c, x, co)
    zo = device(flip3(z), y, x, co)
    z2 = device(flip2(z), y, x, co)
    sib = device(z, y, x, 1 - co)
    partners = (xi, x2, xo, y1, y3, zo, z2, sib)

    x_in = pltpu.make_async_copy(x_hbm, x_ref, local_sems.at[2])
    x_in.start()
    barrier = pltpu.get_barrier_semaphore()
    for partner in partners:
        pl.semaphore_signal(barrier, inc=1, device_id=partner, device_id_type=MESH)

    beta, rho = x // 2, x % 2
    b = 2 * zl + beta
    b_xo = 2 * zl + 1 - beta
    b_zo = 2 * (1 - zl) + beta
    rows = 2 * rho
    rows_flip = 2 - rows
    kg0 = row
    kg1 = 2 * (1 - zh) + co
    m_at, e_at = 3 * (1 - beta), 4 * beta
    m_xo, e_xo = 3 * beta, 4 * (1 - beta)

    def mask_region(q, carry):
        for a in range(4):
            for o in range(3):
                keep = pres_ref[a, o, 0, q].astype(F32)
                xr[3 * q + o, a] = (x_ref[q, a, o].astype(F32) * keep).astype(BF)
                pmask[q, a * 3 + o] = jnp.full((128,), 1.0, F32) * keep
        for i in range(12, 16):
            pmask[q, i] = jnp.zeros((128,), F32)
        return carry

    x_in.wait()
    lax.fori_loop(0, 6, mask_region, 0)
    pl.semaphore_wait(barrier, len(partners))

    started = []

    def send(src, dst, to):
        i = len(started)
        copy = pltpu.make_async_remote_copy(
            src_ref=src, dst_ref=dst, send_sem=send_sems.at[i], recv_sem=recv_sems.at[i],
            device_id=to, device_id_type=MESH,
        )
        copy.start()
        started.append(copy)
        return copy

    def same(ref, to):
        return send(ref, ref, to)

    class Ring:
        def __init__(self, buf, c, wide=1, rows_at=0, count=2):
            self.buf, self.c, self.wide, self.rows = buf, c, wide, pl.ds(rows_at, count)
            self.y1, self.y3 = same(self.at(y), y1), same(self.at(y), y3)

        def at(self, yy, *half):
            return self.buf.at[(pl.ds(4 * yy + self.c, self.wide), slice(None), self.rows, *half)]

        def relay(self):
            self.y1.wait_recv()
            self.a = same(self.at(y1c, pl.ds(0, 64)), y3)
            self.y3.wait_recv()
            self.b = same(self.at(y3c, pl.ds(64, 64)), y1)

        def wait(self):
            self.a.wait_recv()
            self.b.wait_recv()

    def left_of(region, first_row):
        return xr.at[pl.ds(3 * region + 3, 3), pl.ds(first_row, 2)]

    my_left = left.at[4 * y + x]
    own_left_src = left_of(b, rows)
    lp1 = send(left_of(b, rows_flip), my_left, xi)
    lp3 = send(left_of(b_xo, rows_flip), my_left, xo)
    lp2 = send(left_of(b_xo, rows), my_left, x2)
    own_left = pltpu.make_async_copy(own_left_src, my_left, local_sems.at[0])
    own_left.start()

    def native(region, at, size):
        return xr.at[pl.ds(3 * region + 1 + at, size)]

    def panel(j, kg, at=None, size=7):
        return right.at[j, kg] if at is None else right.at[j, kg, pl.ds(at, size)]

    masks = [send(pmask.at[bb + 1], pmask_in.at[i], to) for i, (bb, to) in enumerate(((b, xi), (b_xo, x2), (b_xo, xo)))]
    b_m = send(native(b_zo, m_at, 4), panel(C0, kg0, m_at, 4), zo)
    c_e = send(native(b_xo, e_xo, 3), panel(C3, kg0, e_xo, 3), xo)
    a_m = send(native(b, m_at, 4), panel(C1, kg0, m_at, 4), xi)
    b_e = send(native(b_zo, e_at, 3), panel(C0, kg0, e_at, 3), zo)
    own_right = pltpu.make_async_copy(native(b, 0, 7), panel(C0, kg0), local_sems.at[1])
    own_right.start()
    own_left.wait()
    lp1.wait_recv()
    l_near = Ring(left, 2 * (x // 2), 2)
    a_e = send(native(b, e_at, 3), panel(C1, kg0, e_at, 3), xi)
    sib_0 = send(native(b, 0, 7), panel(C0, kg0), sib)
    lp3.wait_recv()
    lp2.wait_recv()
    l_far = Ring(left, 2 * (1 - x // 2), 2)
    b_m.wait_recv()
    g_m = send(panel(C0, kg1, m_at, 4), panel(C3, kg1, m_xo, 4), xo)
    sib_b_m = same(panel(C0, kg1, m_at, 4), sib)
    c_e.wait_recv()
    h_e = same(panel(C3, kg0, e_at, 3), z2)
    e_e = send(panel(C3, kg0, e_at, 3), panel(C2, kg0, e_at, 3), xi)
    c_m = send(native(b_xo, m_xo, 4), panel(C3, kg0, m_xo, 4), xo)
    sib_c_e = same(panel(C3, kg0, e_at, 3), sib)
    l_near.relay()
    b_e.wait_recv()
    sib_b_e = same(panel(C0, kg1, e_at, 3), sib)
    a_m.wait_recv()
    f_m = send(panel(C1, kg0, m_at, 4), panel(C2, kg0, m_xo, 4), xo)
    sib_a_m = same(panel(C1, kg0, m_at, 4), sib)
    l_far.relay()
    a_e.wait_recv()
    d_m = same(panel(C1, kg0, m_at, 4), z2)
    d_e = same(panel(C1, kg0, e_at, 3), z2)
    sib_a_e = same(panel(C1, kg0, e_at, 3), sib)
    g_m.wait_recv()
    i_m = send(panel(C3, kg1, m_at, 4), panel(C2, kg1, m_at, 4), xi)
    sib_g = same(panel(C3, kg1, m_at, 4), sib)

    def part(j, kg, half):
        return right.at[j, kg, pl.ds(e_at, 3), pl.ds(half, 1 + 2 * half)]

    def square_half(j, first):
        def lhs(kg, d):
            return jnp.concatenate([left[4 * kg + k, d].reshape(256, 128) for k in range(4)], axis=1)

        def block(kg, g):
            return right[j, kg, g].reshape(512, 128)

        if first:
            acc_a[...] = jnp.zeros_like(acc_a)
            acc_b[...] = jnp.zeros_like(acc_b)
            acc_c[...] = jnp.zeros_like(acc_c)
        start = 2 * zh if first else 2 * (1 - zh)

        def group(i, carry):
            kg = start + i
            l_0, l_1, l_2 = lhs(kg, 0), lhs(kg, 1), lhs(kg, 2)
            r = [block(kg, g) for g in range(7)]
            acc_a[...] += jnp.dot(
                jnp.concatenate([l_0, l_1], axis=1),
                jnp.concatenate(
                    [jnp.concatenate([r[0], r[1]], axis=1), jnp.concatenate([r[2], r[3]], axis=1)], axis=0
                ),
                preferred_element_type=F32,
            )
            acc_b[...] += jnp.dot(l_2, jnp.concatenate([r[5], r[6]], axis=1), preferred_element_type=F32)
            acc_c[...] += jnp.dot(l_1, r[4], preferred_element_type=F32)
            return carry

        lax.fori_loop(0, 2, group, 0)

    def kept(j, a, e):
        i = (rows + a) * 3 + e
        return pmask[b + 1, pl.ds(i, 1)] if j == 0 else pmask_in[j - 1, pl.ds(i, 1)]

    def square_store(j, a):
        at = slice(a * 128, a * 128 + 128)
        out = (
            acc_a[at, :128],
            acc_a[at, 128:] + acc_b[at, :128],
            acc_b[at, 128:] + acc_c[at],
        )
        for e in range(3):
            block = out[e] * kept(j, a, e)
            sq32[j, e, a] = block
            sq[4 * y + columns[j], e, a] = block.astype(BF)

    def square_column(j):
        square_half(j, True)
        square_half(j, False)
        square_store(j, 0)
        square_store(j, 1)
        return Ring(sq, columns[j])

    def cube_part(j, first=False, row_at=0, count=2, halves=(0, 1), ys=(0, 1, 2, 3)):
        c, m = columns[j], 128 * count
        at = slice(row_at * 128, row_at * 128 + m)
        for e in range(3):
            offsets = [d for d in range(3) if 0 <= e - d + 1 <= 2]
            lhs = jnp.concatenate(
                [
                    sq[4 * yy + c, d, row_at : row_at + count].reshape(m, 128)
                    for d in offsets for yy in ys
                ],
                axis=1,
            )
            for half in halves:
                rhs = jnp.concatenate(
                    [
                        jnp.concatenate([right[j, yy, 2 * d + e, c] for j in PAIRS[half]], axis=1)
                        for d in offsets for yy in ys
                    ],
                    axis=0,
                )
                part = jnp.dot(lhs, rhs, preferred_element_type=F32)
                if first:
                    cube[e, half, at] = part
                else:
                    cube[e, half, at] += part

    outs = []

    def result_row(a):
        for j in (C2, C1, C3, C0):
            half = 0 if j in PAIRS[0] else 1
            at = PAIRS[half].index(j)
            for e in range(3):
                block = cube[e, half, a * 128 : a * 128 + 128, at * 128 : at * 128 + 128]
                block = (3.0 * sq32[j, e, a] - 2.0 * (block * kept(j, a, e))).astype(BF)
                if j:
                    osend[j, a, e] = block
                else:
                    out_ref[beta, rows + a, e] = block
            if j:
                outs.append(send(osend.at[j, a], out_ref.at[beta, rows + a], (None, xi, x2, xo)[j]))

    def arrived(*copies):
        for copy in copies:
            copy.wait_recv()

    arrived(*masks)
    l_near.wait()
    l_far.wait()
    own_right.wait()
    arrived(sib_0, sib_b_m, sib_b_e)
    s0 = square_column(C0)
    e_e.wait_recv()
    j_e = same(part(C2, kg0, 1), z2)
    sib_e = same(panel(C2, kg0, e_at, 3), sib)
    h_e.wait_recv()
    i_e = send(part(C3, kg1, 0), part(C2, kg1, 0), xi)
    sib_h = same(panel(C3, kg1, e_at, 3), sib)
    c_m.wait_recv()
    sib_c_m = same(panel(C3, kg0, m_at, 4), sib)
    s0.relay()
    arrived(sib_g, sib_h, sib_c_e, sib_c_m)
    s3 = square_column(C3)
    arrived(sib_a_m, sib_a_e)
    square_half(C1, True)
    s0.wait()
    cube_part(C0, True, halves=(0,))
    i_m.wait_recv()
    sib_i_m = same(panel(C2, kg1, m_at, 4), sib)
    d_m.wait_recv()
    sib_d_m = same(panel(C1, kg1, m_at, 4), sib)
    s3.relay()
    d_e.wait_recv()
    sib_d_e = same(panel(C1, kg1, e_at, 3), sib)
    arrived(sib_d_m, sib_d_e)
    square_half(C1, False)
    square_store(C1, 0)
    s1 = [Ring(sq, columns[C1], 1, 0, 1)]
    f_m.wait_recv()
    sib_f = same(panel(C2, kg0, m_at, 4), sib)
    square_store(C1, 1)
    i_e.wait_recv()
    sib_i_e = same(part(C2, kg1, 0), sib)
    j_e.wait_recv()
    sib_j_e = same(part(C2, kg1, 1), sib)
    arrived(sib_f, sib_e)
    square_half(C2, True)
    arrived(sib_i_m, sib_i_e, sib_j_e)
    square_half(C2, False)
    square_store(C2, 0)
    s2 = [Ring(sq, columns[C2], 1, 0, 1)]
    square_store(C2, 1)
    s1[0].relay()
    cube_part(C0, True, halves=(1,))
    s3.wait()
    s2[0].relay()
    s1.append(Ring(sq, columns[C1], 1, 1, 1))
    s2.append(Ring(sq, columns[C2], 1, 1, 1))
    cube_part(C3)
    s1[0].wait()
    cube_part(C1, False, 0, 1)
    cube_part(C2, False, 0, 1, ys=(y, y1c, y3c))
    s2[0].wait()
    cube_part(C2, False, 0, 1, ys=(y2c,))
    result_row(0)
    s1[1].relay()
    s2[1].relay()
    cube_part(C2, False, 1, 1, ys=(y, y1c, y3c))
    s1[1].wait()
    cube_part(C1, False, 1, 1)
    s2[1].wait()
    cube_part(C2, False, 1, 1, ys=(y2c,))
    result_row(1)
    for copy in started:
        if all(copy is not other for other in outs):
            copy.wait_send()
    for copy in outs:
        copy.wait()


def local(x_blocks, present):
    block = jax.ShapeDtypeStruct
    x = x_blocks.reshape(6, 4, 3, 128, 128)
    purified = pl.pallas_call(
        kernel,
        out_shape=block((2, 4, 3, 128, 128), BF),
        in_specs=[pl.BlockSpec(memory_space=pl.ANY), pl.BlockSpec(memory_space=pltpu.SMEM)],
        out_specs=pl.BlockSpec(memory_space=pltpu.VMEM),
        scratch_shapes=[
            pltpu.VMEM((6, 4, 3, 128, 128), BF),
            pltpu.VMEM((18, 4, 128, 128), BF),
            pltpu.VMEM((6, 16, 128), F32),
            pltpu.VMEM((3, 16, 128), F32),
            pltpu.VMEM((16, 3, 2, 128, 128), BF),
            pltpu.VMEM((16, 3, 2, 128, 128), BF),
            pltpu.VMEM((4, 4, 7, 4, 128, 128), BF),
            pltpu.VMEM((4, 3, 2, 128, 128), F32),
            pltpu.VMEM((256, 256), F32),
            pltpu.VMEM((256, 256), F32),
            pltpu.VMEM((256, 128), F32),
            pltpu.VMEM((3, 2, 256, 256), F32),
            pltpu.VMEM((4, 2, 3, 128, 128), BF),
            pltpu.SemaphoreType.DMA((N_SEMS,)),
            pltpu.SemaphoreType.DMA((N_SEMS,)),
            pltpu.SemaphoreType.DMA((3,)),
        ],
        compiler_params=pltpu.CompilerParams(
            collective_id=0, has_side_effects=True, vmem_limit_bytes=44 * 2**20
        ),
        cost_estimate=pl.CostEstimate(flops=7_500_000_000, bytes_accessed=4_000_000, transcendentals=0),
    )(
        pltpu.with_memory_space_constraint(x, pltpu.HBM),
        pltpu.with_memory_space_constraint(present.transpose(1, 2, 3, 0), pltpu.HBM),
    )
    return purified.astype(F32).reshape(2, 4, 3, 1, 128, 128)


def solution(mesh):
    return jax.shard_map(
        local,
        mesh=mesh,
        in_specs=(P(None, "row", None, "col", None, None), P(None, "row", None, "col")),
        out_specs=P("layer", "row", None, "col", None, None),
        check_vma=False,
    )
```
